128 devices in a mesh: freq: 32 (over y, x_hi, z), half: 4 (over x_lo, core).
Axes of the slice: x: 4 (x_hi: 2, x_lo: 2; x = x_hi * 2 + x_lo), y: 4, z: 4, core: 2. Of those that a mesh axis runs over, the one named last changes fastest.
Arguments:
- voltages: bfloat16 [4, 128, 2, 512, 1024], P('half', 'freq'), may hold values from -127 to 127
- scale_exps: int32 [4, 128, 1024], P('half', 'freq'), may hold values from 0 to 3
Outputs:
- visibilities: bfloat16 [1024, 512, 2, 1024], P('half', 'freq')
The draws below stay inside these ranges and needn't reach their ends.
All inputs are finite; a program needn't handle non-finite values.
Results may differ from the reference program's by a relative error of at most 0.0072.
Values may be sent and summed in bfloat16 or wider, within the bound.
A program may use at most 256 MiB of HBM per device.

```python
import math
import jax
import jax.numpy as jnp
from jax import lax

CHANNELS = 512
INPUTS = 1024
HALVES = 4
BLOCKS_HALF = 128


def with_ends(array, own_key, low, top_value):
    spot = [jax.random.randint(jax.random.fold_in(own_key, axis), (), 0, length) for axis, length in enumerate(array.shape)]
    longest = array.shape.index(max(array.shape))
    next_to = spot[:longest] + [(spot[longest] + 1) % array.shape[longest]] + spot[longest + 1:]
    return array.at[tuple(spot)].set(low).at[tuple(next_to)].set(top_value)


def level_of(stream_key, dims, shards, smallest, top_value):
    level = 1.0
    for axis_at, blocks in shards:
        draws = jax.random.uniform(jax.random.fold_in(jax.random.fold_in(stream_key, 6), axis_at), (blocks,), jnp.float32, smallest / len(shards), top_value / len(shards))
        level = level * jnp.repeat(jnp.exp(draws), dims[axis_at] // blocks).reshape((-1,) + (1,) * (len(dims) - 1 - axis_at))
    return level


def centred(key, extent, scale, limit, pieces=(), kind=jnp.bfloat16):
    entries = jax.random.normal(key, extent, jnp.float32) * scale
    if len(pieces) > 0:
        entries = level_of(key, extent, pieces, -0.22, 0.18) * entries
    return jnp.clip(entries, min=-limit, max=limit).astype(kind)


def setup_inputs(seed: int = 0) -> dict:
    arg_keys = jax.random.split(jax.random.key(seed), 3)
    return {
        "voltages": centred(arg_keys[0], (HALVES, BLOCKS_HALF, 2, CHANNELS, INPUTS), 24.0, 127.0, ((0, 4), (1, 32))),
        "scale_exps": with_ends(jax.random.randint(arg_keys[1], (HALVES, BLOCKS_HALF, INPUTS), 0, 4), jax.random.fold_in(arg_keys[1], 1), 0, 3).astype(jnp.int32),
    }


def make_window(count):
    steps = jnp.arange(4 * count, dtype=jnp.float32) + 0.5
    return jnp.sinc(steps / count - 2.0) * (0.5 - 0.5 * jnp.cos(2.0 * math.pi * steps / (4 * count)))

def dft_table(count):
    index = jnp.arange(count, dtype=jnp.int32)
    angle = 2.0 * math.pi / count * (index[:, None] * index[None, :] % count).astype(jnp.float32)
    cosine = jnp.cos(angle)
    sine = jnp.sin(angle)
    upper = jnp.concatenate([cosine, sine], axis=1)
    lower = jnp.concatenate([-sine, cosine], axis=1)
    return jnp.concatenate([upper, lower], axis=0).astype(jnp.bfloat16)

def channelize(scaled):
    taps = make_window(CHANNELS).reshape(4, CHANNELS)
    padded = jnp.concatenate([jnp.zeros((3,) + scaled.shape[1:], jnp.float32), scaled], axis=0)
    filtered = jnp.zeros(scaled.shape, jnp.float32)
    for q in range(4):
        filtered = filtered + padded[q:q + BLOCKS_HALF] * taps[q][None, None, :, None]
    filtered = filtered.astype(jnp.bfloat16).astype(jnp.float32)
    table = dft_table(CHANNELS).astype(jnp.float32)
    flat = filtered.reshape(BLOCKS_HALF, 2 * CHANNELS, INPUTS)
    spectrum = jnp.einsum('pq,tqi->tpi', table, flat) * (1.0 / (256.0 * math.sqrt(CHANNELS)))
    return spectrum.reshape(BLOCKS_HALF, 2, CHANNELS, INPUTS).astype(jnp.bfloat16)

def reference(voltages, scale_exps):

    def one_half(pair):
        volts, exps = pair
        scaled = volts.astype(jnp.float32) * jnp.exp2(exps.astype(jnp.float32))[:, None, None, :]
        scaled = scaled.astype(jnp.bfloat16).astype(jnp.float32)
        return channelize(scaled)
    spectra = lax.map(one_half, (voltages, scale_exps))
    weight = 1.0 / (HALVES * BLOCKS_HALF)

    def one_channel(channel):
        values = lax.dynamic_index_in_dim(spectra, channel, 3, keepdims=False).astype(jnp.float32)
        swapped = jnp.stack([values[:, :, 1], -values[:, :, 0]], axis=2)
        left = jnp.stack([values, swapped], axis=0)
        part = jnp.einsum('phtkr,htkj->hrpj', left, values) * weight
        part = lax.optimization_barrier(part.astype(jnp.bfloat16)).astype(jnp.float32)
        return lax.optimization_barrier(jnp.sum(part, axis=0))
    result = lax.map(one_channel, jnp.arange(CHANNELS, dtype=jnp.int32))
    return jnp.transpose(result, (1, 0, 2, 3)).astype(jnp.bfloat16)
```

```python
import functools
import math

import jax
import jax.numpy as jnp
import ml_dtypes
import numpy as np
from jax import lax
from jax.experimental import pallas as pl
from jax.experimental.pallas import tpu as pltpu
from jax.sharding import PartitionSpec as P

MESH = pl.DeviceIdType.MESH
LANES = 128
COUNT = 512
INPUTS = 1024
CHUNKS = INPUTS // LANES
BLOCKS = 4
PEERS = 16
ROWS = 128


def make_window(count):
    steps = np.arange(4 * count, dtype=np.float64) + 0.5
    window = np.sinc(steps / count - 2.0) * (
        0.5 - 0.5 * np.cos(2.0 * math.pi * steps / (4 * count))
    )
    return window.astype(np.float32)


def dft_table(count):
    index = np.arange(count)
    angle = 2.0 * math.pi / count * (index[:, None] * index[None, :] % count)
    cosine, sine = np.cos(angle), np.sin(angle)
    upper = np.concatenate([cosine, sine], axis=1)
    lower = np.concatenate([-sine, cosine], axis=1)
    table = np.stack([upper, lower], axis=1).reshape(2 * count, 2 * count)
    return table.astype(np.float32).astype(ml_dtypes.bfloat16)


def spread_kernel(
    volts, exps, table, taps, gathered,
    local_in, left_in, right_in, exps_left, exps_right, filtered, regroup, spectra, other,
    in_sem, halo_send, halo_recv, exps_send, exps_recv, own_sem,
    peer_send, peer_recv, pass_send, pass_recv,
):
    f = lax.axis_index("freq")
    h = lax.axis_index("half")
    y, x_hi, z = f // 8, f // 4 % 2, f % 4
    x_lo = h // 2
    me = y * 4 + z
    after = {"freq": (f + 1) % 32, "half": h}
    before = {"freq": (f + 31) % 32, "half": h}
    partner = {"freq": f, "half": (h + 2) % 4}
    sibling = {"freq": f, "half": x_lo * 2 + (h + 1) % 2}
    across = {"freq": y * 8 + (1 - x_hi) * 4 + z, "half": (h + 2) % 4}

    def peer(p):
        py, pz = (y + p // 4) % 4, (z + p % 4) % 4
        return py, pz, {"freq": py * 8 + x_hi * 4 + pz, "half": h}

    def lanes(j):
        return pl.ds(pl.multiple_of(j * LANES, LANES), LANES)

    def load(j):
        return pltpu.make_async_copy(volts.at[:, :, :, lanes(j)], local_in.at[j], in_sem.at[j])

    def halo_right(j):
        return pltpu.make_async_remote_copy(
            volts.at[pl.ds(2, 2), :, :, lanes(j)], left_in.at[j],
            halo_send.at[0, j], halo_recv.at[0, j], device_id=after, device_id_type=MESH,
        )

    def halo_left(j):
        return pltpu.make_async_remote_copy(
            volts.at[pl.ds(0, 1), :, :, lanes(j)], right_in.at[j],
            halo_send.at[1, j], halo_recv.at[1, j], device_id=before, device_id_type=MESH,
        )

    def passing(kind, j, source, slot_h, slot_x, target):
        return pltpu.make_async_remote_copy(
            source, gathered.at[slot_h, slot_x, j],
            pass_send.at[kind, j], pass_recv.at[kind, j], device_id=target, device_id_type=MESH,
        )

    h2, x2 = (h + 2) % 4, 1 - x_hi
    passes = (
        lambda j: passing(0, j, gathered.at[h, x_hi, j], h, x_hi, partner),
        lambda j: passing(1, j, gathered.at[h, x_hi, j], h, x_hi, sibling),
        lambda j: passing(2, j, other.at[j], h, x_hi, across),
        lambda j: passing(3, j, gathered.at[h2, x2, j], h2, x2, partner),
        lambda j: passing(4, j, gathered.at[h2, x2, j], h2, x2, sibling),
        lambda j: passing(5, j, gathered.at[h2, x_hi, j], h2, x_hi, sibling),
        lambda j: passing(6, j, gathered.at[h, x2, j], h, x2, sibling),
    )

    barrier = pltpu.get_barrier_semaphore()

    def greet(p, carry):
        pl.semaphore_signal(barrier, inc=1, device_id=peer(p)[2], device_id_type=MESH)
        return carry

    lax.fori_loop(1, PEERS, greet, 0)
    for device in (after, before, partner, sibling, across):
        pl.semaphore_signal(barrier, inc=1, device_id=device, device_id_type=MESH)
    pl.semaphore_wait(barrier, PEERS - 1 + 5)

    exps_right_going = pltpu.make_async_remote_copy(
        exps, exps_left, exps_send.at[0], exps_recv.at[0], device_id=after, device_id_type=MESH
    )
    exps_left_going = pltpu.make_async_remote_copy(
        exps, exps_right, exps_send.at[1], exps_recv.at[1], device_id=before, device_id_type=MESH
    )
    exps_right_going.start()
    exps_left_going.start()

    def open_chunk(j, carry):
        halo_right(j).start()
        halo_left(j).start()
        load(j).start()
        return carry

    lax.fori_loop(0, CHUNKS, open_chunk, 0)
    exps_right_going.wait_recv()
    exps_left_going.wait_recv()

    not_first = jnp.where(f == 0, 0.0, 1.0).astype(jnp.float32)
    not_last = jnp.where(f == 31, 0.0, 1.0).astype(jnp.float32)

    def compute(j):
        load(j).wait()
        halo_right(j).wait_recv()
        halo_left(j).wait_recv()
        here = jnp.exp2(exps[:, lanes(j)].astype(jnp.float32))
        left = jnp.exp2(exps_left[:, lanes(j)].astype(jnp.float32)) * not_first
        right = jnp.exp2(exps_right[:, lanes(j)].astype(jnp.float32))
        factor = [left[2:3], left[3:4]] + [here[b : b + 1] for b in range(4)] + [right[0:1]]

        for k in range(2):
            def filter_rows(i, carry):
                rows = pl.ds(pl.multiple_of(i * 32, 32), 32)
                blocks = [left_in[j, b, k, rows, :] for b in range(2)]
                blocks += [local_in[j, b, k, rows, :] for b in range(4)]
                blocks += [right_in[j, 0, k, rows, :]]
                scaled = [b.astype(jnp.float32) * s for b, s in zip(blocks, factor)]
                tap = [taps[q, rows, :] for q in range(4)]
                for t in range(BLOCKS):
                    total = scaled[t] * tap[0] + scaled[t + 1] * tap[1] + scaled[t + 2] * tap[2]
                    if t == BLOCKS - 1:
                        total = total * not_last
                    total = total + scaled[t + 3] * tap[3]
                    filtered[pl.ds(pl.multiple_of(k * COUNT + i * 32, 32), 32),
                             t * LANES : (t + 1) * LANES] = total.astype(jnp.bfloat16)
                return carry

            lax.fori_loop(0, COUNT // 32, filter_rows, 0)

        def transform(m, carry):
            result = jnp.dot(
                table[pl.ds(pl.multiple_of(m * 256, 256), 256), :], filtered[...],
                preferred_element_type=jnp.float32,
            ) * (1.0 / (256.0 * math.sqrt(COUNT)))
            for t in range(BLOCKS):
                regroup[pl.ds(t, 256, stride=BLOCKS), :] = result[:, t * LANES : (t + 1) * LANES]
            spectra[j, pl.ds(m * 8, 8)] = regroup[...].astype(jnp.bfloat16).reshape(8, ROWS, LANES)
            return carry

        lax.fori_loop(0, 4, transform, 0)

    def own_copies(j):
        mine = y * 8 + x_hi * 4 + z
        rest = y * 8 + x2 * 4 + z
        return (
            pltpu.make_async_copy(spectra.at[j, mine], gathered.at[h, x_hi, j, me], own_sem.at[0, j]),
            pltpu.make_async_copy(spectra.at[j, rest], other.at[j, me], own_sem.at[1, j]),
        )

    def send_peers(j):
        for copy in own_copies(j):
            copy.start()

        def one(p, carry):
            py, pz, device = peer(p)
            pltpu.make_async_remote_copy(
                spectra.at[j, py * 8 + x_hi * 4 + pz], gathered.at[h, x_hi, j, me],
                peer_send.at[0, j], peer_recv.at[0, j], device_id=device, device_id_type=MESH,
            ).start()
            pltpu.make_async_remote_copy(
                spectra.at[j, py * 8 + x2 * 4 + pz], other.at[j, me],
                peer_send.at[1, j], peer_recv.at[1, j], device_id=device, device_id_type=MESH,
            ).start()
            return carry

        lax.fori_loop(1, PEERS, one, 0)

    def take(ref, sem):
        pltpu.make_async_copy(ref, ref, sem).wait()

    def wait_peers(j):
        for copy in own_copies(j):
            copy.wait()
        take(gathered.at[h, x_hi, j, pl.ds(0, PEERS - 1)], peer_recv.at[0, j])
        take(other.at[j, pl.ds(0, PEERS - 1)], peer_recv.at[1, j])

    def step(j, carry):
        @pl.when(j < CHUNKS)
        def _():
            compute(j)
            send_peers(j)

        @pl.when((j >= 1) & (j < CHUNKS + 1))
        def _():
            i = j - 1
            wait_peers(i)
            passes[2](i).start()
            passes[0](i).start()
            passes[1](i).start()

        @pl.when((j >= 2) & (j < CHUNKS + 2))
        def _():
            i = j - 2
            passes[2](i).wait_recv()
            passes[3](i).start()
            passes[4](i).start()
            passes[0](i).wait_recv()
            passes[5](i).start()

        @pl.when(j >= 3)
        def _():
            i = j - 3
            passes[3](i).wait_recv()
            passes[6](i).start()

        return carry

    lax.fori_loop(0, CHUNKS + 3, step, 0)

    def finish(j, carry):
        for kind in (1, 4, 5, 6):
            passes[kind](j).wait_recv()
        for kind in range(7):
            passes[kind](j).wait_send()
        halo_right(j).wait_send()
        halo_left(j).wait_send()
        take(spectra.at[j, pl.ds(0, PEERS - 1)], peer_send.at[0, j])
        take(spectra.at[j, pl.ds(0, PEERS - 1)], peer_send.at[1, j])
        return carry

    lax.fori_loop(0, CHUNKS, finish, 0)
    exps_right_going.wait_send()
    exps_left_going.wait_send()


def spread(volts, exps):
    table = jnp.asarray(dft_table(COUNT))
    taps = jnp.asarray(
        np.ascontiguousarray(
            np.broadcast_to(make_window(COUNT).reshape(4, COUNT, 1), (4, COUNT, LANES))
        )
    )
    in_vmem = pl.BlockSpec(memory_space=pltpu.VMEM)
    dma = pltpu.SemaphoreType.DMA
    return pl.pallas_call(
        spread_kernel,
        out_shape=jax.ShapeDtypeStruct((4, 2, CHUNKS, PEERS, ROWS, LANES), jnp.bfloat16),
        in_specs=[pl.BlockSpec(memory_space=pl.ANY), in_vmem, in_vmem, in_vmem],
        out_specs=pl.BlockSpec(memory_space=pl.ANY),
        scratch_shapes=[
            pltpu.VMEM((CHUNKS, BLOCKS, 2, COUNT, LANES), jnp.bfloat16),
            pltpu.VMEM((CHUNKS, 2, 2, COUNT, LANES), jnp.bfloat16),
            pltpu.VMEM((CHUNKS, 1, 2, COUNT, LANES), jnp.bfloat16),
            pltpu.VMEM((BLOCKS, INPUTS), jnp.int32),
            pltpu.VMEM((BLOCKS, INPUTS), jnp.int32),
            pltpu.VMEM((2 * COUNT, BLOCKS * LANES), jnp.bfloat16),
            pltpu.VMEM((256 * BLOCKS, LANES), jnp.float32),
            pltpu.VMEM((CHUNKS, 32, ROWS, LANES), jnp.bfloat16),
            pltpu.VMEM((CHUNKS, PEERS, ROWS, LANES), jnp.bfloat16),
            dma((CHUNKS,)),
            dma((2, CHUNKS)),
            dma((2, CHUNKS)),
            dma((2,)),
            dma((2,)),
            dma((2, CHUNKS)),
            dma((2, CHUNKS)),
            dma((2, CHUNKS)),
            dma((7, CHUNKS)),
            dma((7, CHUNKS)),
        ],
        compiler_params=pltpu.CompilerParams(
            collective_id=0, has_side_effects=True, vmem_limit_bytes=56 * 2**20
        ),
        cost_estimate=pl.CostEstimate(
            flops=8 * 2**30, bytes_accessed=50 * 2**20, transcendentals=0
        ),
    )(volts, exps, table, taps)


def correlate_kernel(spectra, out, values, left):
    half = lax.axis_index("half")
    sources = 8 * PEERS
    for u in range(CHUNKS):
        wide = spectra[:, u].astype(jnp.float32).reshape(sources, 2, 8, LANES)
        for c in range(2):
            values[c, :, u * LANES : (u + 1) * LANES] = (
                wide[:, c].reshape(sources * 8, LANES).astype(jnp.bfloat16)
            )
    sign = jnp.where(lax.broadcasted_iota(jnp.int32, (1, 8, LANES), 1) < 4, 1.0, -1.0)
    for u in range(2):
        wide = spectra[:, 2 * half + u].astype(jnp.float32).reshape(sources, 2, 8, LANES)
        for c in range(2):
            plain = wide[:, c]
            swapped = pltpu.roll(plain, 4, 1) * sign
            at = u * LANES
            left[c, :, at : at + LANES] = plain.reshape(sources * 8, LANES).astype(jnp.bfloat16)
            at = 256 + u * LANES
            left[c, :, at : at + LANES] = swapped.reshape(sources * 8, LANES).astype(jnp.bfloat16)
    for c in range(2):
        result = lax.dot_general(
            left[c], values[c], (((0,), (0,)), ((), ())), preferred_element_type=jnp.float32
        ) * (1.0 / 512.0)
        out[:, c, 0, :] = result[:256].astype(jnp.bfloat16)
        out[:, c, 1, :] = result[256:].astype(jnp.bfloat16)


def correlate(spectra):
    return pl.pallas_call(
        correlate_kernel,
        grid=(8,),
        out_shape=jax.ShapeDtypeStruct((256, 16, 2, INPUTS), jnp.bfloat16),
        in_specs=[pl.BlockSpec((8, CHUNKS, PEERS, 16, LANES), lambda i: (0, 0, 0, i, 0))],
        out_specs=pl.BlockSpec((256, 2, 2, INPUTS), lambda i: (0, i, 0, 0)),
        scratch_shapes=[
            pltpu.VMEM((2, 1024, INPUTS), jnp.bfloat16),
            pltpu.VMEM((2, 1024, 512), jnp.bfloat16),
        ],
        compiler_params=pltpu.CompilerParams(vmem_limit_bytes=56 * 2**20),
        cost_estimate=pl.CostEstimate(
            flops=16 * 2**30, bytes_accessed=48 * 2**20, transcendentals=0
        ),
    )(spectra)


def per_device(voltages, scale_exps):
    gathered = spread(voltages[0], scale_exps[0])
    return correlate(gathered.reshape(8, CHUNKS, PEERS, ROWS, LANES))


def solution(mesh):
    return jax.shard_map(
        per_device,
        mesh=mesh,
        in_specs=(P("half", "freq", None, None, None), P("half", "freq", None)),
        out_specs=P("half", "freq", None, None),
        check_vma=False,
    )
```

```python
import functools
import math

import jax
import jax.numpy as jnp
import ml_dtypes
import numpy as np
from jax import lax
from jax.experimental import pallas as pl
from jax.experimental.pallas import tpu as pltpu
from jax.sharding import PartitionSpec as P

MESH = pl.DeviceIdType.MESH
LANES = 128
COUNT = 512
INPUTS = 1024
CHUNKS = INPUTS // LANES
BLOCKS = 4
PEERS = 16
ROWS = 128


def make_window(count):
    steps = np.arange(4 * count, dtype=np.float64) + 0.5
    window = np.sinc(steps / count - 2.0) * (
        0.5 - 0.5 * np.cos(2.0 * math.pi * steps / (4 * count))
    )
    return window.astype(np.float32)


def dft_table(count):
    index = np.arange(count)
    angle = 2.0 * math.pi / count * (index[:, None] * index[None, :] % count)
    cosine, sine = np.cos(angle), np.sin(angle)
    upper = np.concatenate([cosine, sine], axis=1)
    lower = np.concatenate([-sine, cosine], axis=1)
    table = np.stack([upper, lower], axis=1).reshape(2 * count, 2 * count)
    return table.astype(np.float32).astype(ml_dtypes.bfloat16)


def spread_kernel(
    volts, exps, table, taps, gathered,
    window, relay, exps_left, exps_right, filtered, regroup, spectra, other,
    in_sem, halo_send, halo_recv, relay_send, relay_recv, exps_send, exps_recv, own_sem,
    peer_send, peer_recv, pass_send, pass_recv,
):
    f = lax.axis_index("freq")
    h = lax.axis_index("half")
    y, x_hi, z = f // 8, f // 4 % 2, f % 4
    x_lo = h // 2
    me = y * 4 + z
    after = {"freq": (f + 1) % 32, "half": h}
    before = {"freq": (f + 31) % 32, "half": h}
    partner = {"freq": f, "half": (h + 2) % 4}
    sibling = {"freq": f, "half": x_lo * 2 + (h + 1) % 2}
    across = {"freq": y * 8 + (1 - x_hi) * 4 + z, "half": (h + 2) % 4}

    def peer(p):
        py, pz = (y + p // 4) % 4, (z + p % 4) % 4
        return py, pz, {"freq": py * 8 + x_hi * 4 + pz, "half": h}

    def lanes(j):
        return pl.ds(pl.multiple_of(j * LANES, LANES), LANES)

    wide = h % 2

    def load(j):
        return pltpu.make_async_copy(
            volts.at[:, :, :, lanes(j)], window.at[j, pl.ds(2 - wide, BLOCKS)], in_sem.at[j]
        )

    halo_block = (3, 2, 0, 1)

    def place(kind, j):
        return (1 - wide, 0, 6 - wide, 6)[kind]

    def row(kind, j):
        return (3 + j) % 4 if kind < 2 else j % 4

    def halo(kind, j):
        return pltpu.make_async_remote_copy(
            volts.at[halo_block[kind], :, :, lanes(j)], window.at[j, place(kind, j)],
            halo_send.at[kind, j], halo_recv.at[kind, j],
            device_id=after if kind < 2 else before, device_id_type=MESH,
        )

    def halo_to_relay(kind, j):
        return pltpu.make_async_remote_copy(
            volts.at[halo_block[kind], :, :, lanes(j)], relay.at[kind, j // 4],
            halo_send.at[kind, j], relay_recv.at[kind, j // 4],
            device_id={"freq": f - z + row(kind, j), "half": h}, device_id_type=MESH,
        )

    def halo_from_relay(kind, j):
        beyond = (f - z + 4) % 32 if kind < 2 else (f - z + 31) % 32
        return pltpu.make_async_remote_copy(
            relay.at[kind, j // 4], window.at[j, place(kind, j)],
            relay_send.at[kind, j // 4], halo_recv.at[kind, j],
            device_id={"freq": beyond, "half": h}, device_id_type=MESH,
        )

    edge = (3, 3, 0, 0)

    def each_kind(j, act):
        for kind in range(4):
            if kind % 2 == 0:
                act(kind)
            else:
                pl.when(wide == kind // 2)(functools.partial(act, kind))

    def start_halo(j):
        def act(kind):
            direct = (z != edge[kind]) | (row(kind, j) == edge[kind])
            pl.when(direct)(lambda: halo(kind, j).start())
            pl.when(jnp.logical_not(direct))(lambda: halo_to_relay(kind, j).start())

        each_kind(j, act)

    def relays(kind, j):
        return (z != edge[kind]) & (row(kind, j) == z)

    def relay_halo(j):
        def act(kind):
            @pl.when(relays(kind, j))
            def _():
                halo_to_relay(kind, j).wait_recv()
                halo_from_relay(kind, j).start()

        each_kind(j, act)

    def wait_halo(j):
        each_kind(j, lambda kind: halo(kind, j).wait_recv())

    def finish_halo(j):
        def act(kind):
            halo(kind, j).wait_send()
            pl.when(relays(kind, j))(lambda: halo_from_relay(kind, j).wait_send())

        each_kind(j, act)

    def passing(kind, j, source, slot_h, slot_x, target):
        return pltpu.make_async_remote_copy(
            source, gathered.at[slot_h, slot_x, j],
            pass_send.at[kind, j], pass_recv.at[kind, j], device_id=target, device_id_type=MESH,
        )

    h2, x2 = (h + 2) % 4, 1 - x_hi
    passes = (
        lambda j: passing(0, j, gathered.at[h, x_hi, j], h, x_hi, partner),
        lambda j: passing(1, j, gathered.at[h, x_hi, j], h, x_hi, sibling),
        lambda j: passing(2, j, other.at[j], h, x_hi, across),
        lambda j: passing(3, j, gathered.at[h2, x2, j], h2, x2, partner),
        lambda j: passing(4, j, gathered.at[h2, x2, j], h2, x2, sibling),
        lambda j: passing(5, j, gathered.at[h2, x_hi, j], h2, x_hi, sibling),
        lambda j: passing(6, j, gathered.at[h, x2, j], h, x2, sibling),
    )

    barrier = pltpu.get_barrier_semaphore()

    def greet(p, carry):
        pl.semaphore_signal(barrier, inc=1, device_id=peer(p)[2], device_id_type=MESH)
        return carry

    lax.fori_loop(1, PEERS, greet, 0)
    for device in (after, before, partner, sibling, across):
        pl.semaphore_signal(barrier, inc=1, device_id=device, device_id_type=MESH)
    for step_back in (2, 3, 4):
        @pl.when(z == 0)
        def _():
            device = {"freq": (f + 32 - step_back) % 32, "half": h}
            pl.semaphore_signal(barrier, inc=1, device_id=device, device_id_type=MESH)

        @pl.when(z == 3)
        def _():
            device = {"freq": (f + step_back) % 32, "half": h}
            pl.semaphore_signal(barrier, inc=1, device_id=device, device_id_type=MESH)

    edges = jnp.where(z < 3, 1, 0) + jnp.where(z > 0, 1, 0)
    pl.semaphore_wait(barrier, PEERS - 1 + 5 + edges)

    exps_right_going = pltpu.make_async_remote_copy(
        exps, exps_left, exps_send.at[0], exps_recv.at[0], device_id=after, device_id_type=MESH
    )
    exps_left_going = pltpu.make_async_remote_copy(
        exps, exps_right, exps_send.at[1], exps_recv.at[1], device_id=before, device_id_type=MESH
    )
    exps_right_going.start()
    exps_left_going.start()
    start_halo(0)

    def open_chunk(j, carry):
        load(j).start()
        return carry

    lax.fori_loop(0, CHUNKS, open_chunk, 0)
    exps_right_going.wait_recv()
    exps_left_going.wait_recv()

    not_first = jnp.where(f == 0, 0.0, 1.0).astype(jnp.float32)

    def compute(j):
        shift = wide
        keep_0 = jnp.where((f == 31) & (shift == 0), 0.0, 1.0).astype(jnp.float32)
        keep_1 = jnp.where((f == 31) & (shift == 1), 0.0, 1.0).astype(jnp.float32)
        keep = jnp.where(f == 31, 0.0, 1.0).astype(jnp.float32)
        here = jnp.exp2(exps[:, lanes(j)].astype(jnp.float32))
        left = jnp.exp2(exps_left[:, lanes(j)].astype(jnp.float32)) * not_first
        right = jnp.exp2(exps_right[:, lanes(j)].astype(jnp.float32))
        line = [left[2:3], left[3:4]] + [here[b : b + 1] for b in range(4)] + [right[0:1], right[1:2]]
        factor = [jnp.where(shift == 0, line[b], line[b + 1]) for b in range(7)]

        for k in range(2):
            def filter_rows(i, carry):
                rows = pl.ds(pl.multiple_of(i * 32, 32), 32)
                scaled = [window[j, b, k, rows, :].astype(jnp.float32) * factor[b] for b in range(7)]
                tap = [taps[q, rows, :] for q in range(4)]
                for t in range(BLOCKS):
                    if t < 2:
                        total = scaled[t] * tap[0] + scaled[t + 1] * tap[1] + scaled[t + 2] * tap[2]
                    elif t == 2:
                        total = scaled[t] * tap[0] + scaled[t + 1] * tap[1] + scaled[t + 2] * tap[2]
                        total = total * keep_1
                    else:
                        total = (scaled[t] * tap[0] + scaled[t + 1] * tap[1]) * keep
                        total = total + scaled[t + 2] * tap[2] * keep_0
                    total = total + scaled[t + 3] * tap[3]
                    filtered[pl.ds(pl.multiple_of(k * COUNT + i * 32, 32), 32),
                             t * LANES : (t + 1) * LANES] = total.astype(jnp.bfloat16)
                return carry

            lax.fori_loop(0, COUNT // 32, filter_rows, 0)

        def transform(m, carry):
            result = jnp.dot(
                table[pl.ds(pl.multiple_of(m * 256, 256), 256), :], filtered[...],
                preferred_element_type=jnp.float32,
            ) * (1.0 / (256.0 * math.sqrt(COUNT)))
            for t in range(BLOCKS):
                regroup[pl.ds(t, 256, stride=BLOCKS), :] = result[:, t * LANES : (t + 1) * LANES]
            spectra[j, pl.ds(m * 8, 8)] = regroup[...].astype(jnp.bfloat16).reshape(8, ROWS, LANES)
            return carry

        lax.fori_loop(0, 4, transform, 0)

    def own_copies(j):
        mine = y * 8 + x_hi * 4 + z
        rest = y * 8 + x2 * 4 + z
        return (
            pltpu.make_async_copy(spectra.at[j, mine], gathered.at[h, x_hi, j, me], own_sem.at[0, j]),
            pltpu.make_async_copy(spectra.at[j, rest], other.at[j, me], own_sem.at[1, j]),
        )

    def send_peers(j):
        for copy in own_copies(j):
            copy.start()

        def one(p, carry):
            py, pz, device = peer(p)
            pltpu.make_async_remote_copy(
                spectra.at[j, py * 8 + x_hi * 4 + pz], gathered.at[h, x_hi, j, me],
                peer_send.at[0, j], peer_recv.at[0, j], device_id=device, device_id_type=MESH,
            ).start()
            pltpu.make_async_remote_copy(
                spectra.at[j, py * 8 + x2 * 4 + pz], other.at[j, me],
                peer_send.at[1, j], peer_recv.at[1, j], device_id=device, device_id_type=MESH,
            ).start()
            return carry

        lax.fori_loop(1, PEERS, one, 0)

    def take(ref, sem):
        pltpu.make_async_copy(ref, ref, sem).wait()

    def wait_peers(j):
        for copy in own_copies(j):
            copy.wait()
        take(gathered.at[h, x_hi, j, pl.ds(0, PEERS - 1)], peer_recv.at[0, j])
        take(other.at[j, pl.ds(0, PEERS - 1)], peer_recv.at[1, j])

    def step(j, carry):
        @pl.when(j < CHUNKS)
        def _():
            load(j).wait()
            wait_halo(j)

            @pl.when(j == 0)
            def _():
                start_halo(1)

            @pl.when(j + 2 < CHUNKS)
            def _():
                start_halo(j + 2)

            compute(j)
            send_peers(j)

        @pl.when(j + 1 < CHUNKS)
        def _():
            relay_halo(j + 1)

        @pl.when((j >= 1) & (j < CHUNKS + 1))
        def _():
            i = j - 1
            wait_peers(i)
            passes[2](i).start()
            passes[0](i).start()
            passes[1](i).start()

        @pl.when((j >= 2) & (j < CHUNKS + 2))
        def _():
            i = j - 2
            passes[2](i).wait_recv()
            passes[3](i).start()
            passes[4](i).start()
            passes[0](i).wait_recv()
            passes[5](i).start()

        @pl.when(j >= 3)
        def _():
            i = j - 3
            passes[3](i).wait_recv()
            passes[6](i).start()

        return carry

    lax.fori_loop(0, CHUNKS + 3, step, 0)

    def finish(j, carry):
        for kind in (1, 4, 5, 6):
            passes[kind](j).wait_recv()
        for kind in range(7):
            passes[kind](j).wait_send()
        finish_halo(j)
        take(spectra.at[j, pl.ds(0, PEERS - 1)], peer_send.at[0, j])
        take(spectra.at[j, pl.ds(0, PEERS - 1)], peer_send.at[1, j])
        return carry

    lax.fori_loop(0, CHUNKS, finish, 0)
    exps_right_going.wait_send()
    exps_left_going.wait_send()


def spread(volts, exps):
    table = jnp.asarray(dft_table(COUNT))
    taps = jnp.asarray(
        np.ascontiguousarray(
            np.broadcast_to(make_window(COUNT).reshape(4, COUNT, 1), (4, COUNT, LANES))
        )
    )
    in_vmem = pl.BlockSpec(memory_space=pltpu.VMEM)
    dma = pltpu.SemaphoreType.DMA
    return pl.pallas_call(
        spread_kernel,
        out_shape=jax.ShapeDtypeStruct((4, 2, CHUNKS, PEERS, ROWS, LANES), jnp.bfloat16),
        in_specs=[pl.BlockSpec(memory_space=pl.ANY), in_vmem, in_vmem, in_vmem],
        out_specs=pl.BlockSpec(memory_space=pl.ANY),
        scratch_shapes=[
            pltpu.VMEM((CHUNKS, 7, 2, COUNT, LANES), jnp.bfloat16),
            pltpu.VMEM((4, 2, 2, COUNT, LANES), jnp.bfloat16),
            pltpu.VMEM((BLOCKS, INPUTS), jnp.int32),
            pltpu.VMEM((BLOCKS, INPUTS), jnp.int32),
            pltpu.VMEM((2 * COUNT, BLOCKS * LANES), jnp.bfloat16),
            pltpu.VMEM((256 * BLOCKS, LANES), jnp.float32),
            pltpu.VMEM((CHUNKS, 32, ROWS, LANES), jnp.bfloat16),
            pltpu.VMEM((CHUNKS, PEERS, ROWS, LANES), jnp.bfloat16),
            dma((CHUNKS,)),
            dma((4, CHUNKS)),
            dma((4, CHUNKS)),
            dma((4, 2)),
            dma((4, 2)),
            dma((2,)),
            dma((2,)),
            dma((2, CHUNKS)),
            dma((2, CHUNKS)),
            dma((2, CHUNKS)),
            dma((7, CHUNKS)),
            dma((7, CHUNKS)),
        ],
        compiler_params=pltpu.CompilerParams(
            collective_id=0, has_side_effects=True, vmem_limit_bytes=56 * 2**20
        ),
        cost_estimate=pl.CostEstimate(
            flops=8 * 2**30, bytes_accessed=50 * 2**20, transcendentals=0
        ),
    )(volts, exps, table, taps)


def correlate_kernel(spectra, out, values, left):
    half = lax.axis_index("half")
    sources = 8 * PEERS
    for u in range(CHUNKS):
        wide = spectra[:, u].astype(jnp.float32).reshape(sources, 2, 8, LANES)
        for c in range(2):
            values[c, :, u * LANES : (u + 1) * LANES] = (
                wide[:, c].reshape(sources * 8, LANES).astype(jnp.bfloat16)
            )
    sign = jnp.where(lax.broadcasted_iota(jnp.int32, (1, 8, LANES), 1) < 4, 1.0, -1.0)
    for u in range(2):
        wide = spectra[:, 2 * half + u].astype(jnp.float32).reshape(sources, 2, 8, LANES)
        for c in range(2):
            plain = wide[:, c]
            swapped = pltpu.roll(plain, 4, 1) * sign
            at = u * LANES
            left[c, :, at : at + LANES] = plain.reshape(sources * 8, LANES).astype(jnp.bfloat16)
            at = 256 + u * LANES
            left[c, :, at : at + LANES] = swapped.reshape(sources * 8, LANES).astype(jnp.bfloat16)
    for c in range(2):
        result = lax.dot_general(
            left[c], values[c], (((0,), (0,)), ((), ())), preferred_element_type=jnp.float32
        ) * (1.0 / 512.0)
        out[:, c, 0, :] = result[:256].astype(jnp.bfloat16)
        out[:, c, 1, :] = result[256:].astype(jnp.bfloat16)


def correlate(spectra):
    return pl.pallas_call(
        correlate_kernel,
        grid=(8,),
        out_shape=jax.ShapeDtypeStruct((256, 16, 2, INPUTS), jnp.bfloat16),
        in_specs=[pl.BlockSpec((8, CHUNKS, PEERS, 16, LANES), lambda i: (0, 0, 0, i, 0))],
        out_specs=pl.BlockSpec((256, 2, 2, INPUTS), lambda i: (0, i, 0, 0)),
        scratch_shapes=[
            pltpu.VMEM((2, 1024, INPUTS), jnp.bfloat16),
            pltpu.VMEM((2, 1024, 512), jnp.bfloat16),
        ],
        compiler_params=pltpu.CompilerParams(vmem_limit_bytes=56 * 2**20),
        cost_estimate=pl.CostEstimate(
            flops=16 * 2**30, bytes_accessed=48 * 2**20, transcendentals=0
        ),
    )(spectra)


def per_device(voltages, scale_exps):
    gathered = spread(voltages[0], scale_exps[0])
    return correlate(gathered.reshape(8, CHUNKS, PEERS, ROWS, LANES))


def solution(mesh):
    return jax.shard_map(
        per_device,
        mesh=mesh,
        in_specs=(P("half", "freq", None, None, None), P("half", "freq", None)),
        out_specs=P("half", "freq", None, None),
        check_vma=False,
    )
```

```python
import functools
import math

import jax
import jax.numpy as jnp
import ml_dtypes
import numpy as np
from jax import lax
from jax.experimental import pallas as pl
from jax.experimental.pallas import tpu as pltpu
from jax.sharding import PartitionSpec as P

MESH = pl.DeviceIdType.MESH
LANES = 128
COUNT = 512
INPUTS = 1024
CHUNKS = INPUTS // LANES
BLOCKS = 4
PEERS = 16
ROWS = 128


def make_window(count):
    steps = np.arange(4 * count, dtype=np.float64) + 0.5
    window = np.sinc(steps / count - 2.0) * (
        0.5 - 0.5 * np.cos(2.0 * math.pi * steps / (4 * count))
    )
    return window.astype(np.float32)


def dft_table(count):
    index = np.arange(count)
    angle = 2.0 * math.pi / count * (index[:, None] * index[None, :] % count)
    cosine, sine = np.cos(angle), np.sin(angle)
    upper = np.concatenate([cosine, sine], axis=1)
    lower = np.concatenate([-sine, cosine], axis=1)
    table = np.stack([upper, lower], axis=1).reshape(2 * count, 2 * count)
    return table.astype(np.float32).astype(ml_dtypes.bfloat16)


def spread_kernel(
    volts, exps, table, taps, gathered,
    window, relay, exps_left, exps_right, filtered, regroup, spectra, other,
    in_sem, halo_send, halo_recv, relay_send, relay_recv, exps_send, exps_recv, own_sem,
    peer_send, peer_recv, pass_send, pass_recv,
):
    f = lax.axis_index("freq")
    h = lax.axis_index("half")
    y, x_hi, z = f // 8, f // 4 % 2, f % 4
    x_lo = h // 2
    me = y * 4 + z
    after = {"freq": (f + 1) % 32, "half": h}
    before = {"freq": (f + 31) % 32, "half": h}
    partner = {"freq": f, "half": (h + 2) % 4}
    sibling = {"freq": f, "half": x_lo * 2 + (h + 1) % 2}
    across = {"freq": y * 8 + (1 - x_hi) * 4 + z, "half": (h + 2) % 4}

    def peer(p):
        py, pz = (y + p // 4) % 4, (z + p % 4) % 4
        return py, pz, {"freq": py * 8 + x_hi * 4 + pz, "half": h}

    def lanes(j):
        return pl.ds(pl.multiple_of(j * LANES, LANES), LANES)

    wide = h % 2

    def load(j):
        return pltpu.make_async_copy(
            volts.at[:, :, :, lanes(j)], window.at[j, pl.ds(2 - wide, BLOCKS)], in_sem.at[j]
        )

    halo_block = (3, 2, 0, 1)

    def place(kind, j):
        return (1 - wide, 0, 6 - wide, 6)[kind]

    edge = (3, 3, 0, 0)
    part = COUNT // 4

    def halo(kind, j):
        return pltpu.make_async_remote_copy(
            volts.at[halo_block[kind], :, :, lanes(j)], window.at[j, place(kind, j)],
            halo_send.at[kind, j], halo_recv.at[kind, j],
            device_id=after if kind < 2 else before, device_id_type=MESH,
        )

    def halo_part(kind, j, q):
        rows = pl.ds(q * part, part)
        source = volts.at[halo_block[kind], :, rows, lanes(j)]
        if q == edge[kind]:
            return pltpu.make_async_remote_copy(
                source, window.at[j, place(kind, j), :, rows],
                halo_send.at[kind, j], halo_recv.at[kind, j],
                device_id=after if kind < 2 else before, device_id_type=MESH,
            )
        return pltpu.make_async_remote_copy(
            source, relay.at[kind, j], halo_send.at[kind, j], relay_recv.at[kind, j],
            device_id={"freq": f - z + q, "half": h}, device_id_type=MESH,
        )

    def halo_from_relay(kind, j):
        beyond = (f - z + 4) % 32 if kind < 2 else (f - z + 31) % 32
        rows = pl.ds(pl.multiple_of(z * part, part), part)
        return pltpu.make_async_remote_copy(
            relay.at[kind, j], window.at[j, place(kind, j), :, rows],
            relay_send.at[kind, j], halo_recv.at[kind, j],
            device_id={"freq": beyond, "half": h}, device_id_type=MESH,
        )

    def each_kind(act):
        for kind in range(4):
            if kind % 2 == 0:
                act(kind)
            else:
                pl.when(wide == kind // 2)(functools.partial(act, kind))

    def start_halo(j):
        def act(kind):
            pl.when(z != edge[kind])(lambda: halo(kind, j).start())

            @pl.when(z == edge[kind])
            def _():
                for q in range(4):
                    halo_part(kind, j, q).start()

        each_kind(act)

    def relay_halo(j):
        def act(kind):
            @pl.when(z != edge[kind])
            def _():
                pltpu.make_async_copy(
                    relay.at[kind, j], relay.at[kind, j], relay_recv.at[kind, j]
                ).wait()
                halo_from_relay(kind, j).start()

        each_kind(act)

    def wait_halo(j):
        each_kind(lambda kind: halo(kind, j).wait_recv())

    def finish_halo(j):
        def act(kind):
            halo(kind, j).wait_send()
            pl.when(z != edge[kind])(lambda: halo_from_relay(kind, j).wait_send())

        each_kind(act)

    def passing(kind, j, source, slot_h, slot_x, target):
        return pltpu.make_async_remote_copy(
            source, gathered.at[slot_h, slot_x, j],
            pass_send.at[kind, j], pass_recv.at[kind, j], device_id=target, device_id_type=MESH,
        )

    h2, x2 = (h + 2) % 4, 1 - x_hi
    passes = (
        lambda j: passing(0, j, gathered.at[h, x_hi, j], h, x_hi, partner),
        lambda j: passing(1, j, gathered.at[h, x_hi, j], h, x_hi, sibling),
        lambda j: passing(2, j, other.at[j], h, x_hi, across),
        lambda j: passing(3, j, gathered.at[h2, x2, j], h2, x2, partner),
        lambda j: passing(4, j, gathered.at[h2, x2, j], h2, x2, sibling),
        lambda j: passing(5, j, gathered.at[h2, x_hi, j], h2, x_hi, sibling),
        lambda j: passing(6, j, gathered.at[h, x2, j], h, x2, sibling),
    )

    barrier = pltpu.get_barrier_semaphore()

    def greet(p, carry):
        pl.semaphore_signal(barrier, inc=1, device_id=peer(p)[2], device_id_type=MESH)
        return carry

    lax.fori_loop(1, PEERS, greet, 0)
    for device in (after, before, partner, sibling, across):
        pl.semaphore_signal(barrier, inc=1, device_id=device, device_id_type=MESH)
    for step_back in (2, 3, 4):
        @pl.when(z == 0)
        def _():
            device = {"freq": (f + 32 - step_back) % 32, "half": h}
            pl.semaphore_signal(barrier, inc=1, device_id=device, device_id_type=MESH)

        @pl.when(z == 3)
        def _():
            device = {"freq": (f + step_back) % 32, "half": h}
            pl.semaphore_signal(barrier, inc=1, device_id=device, device_id_type=MESH)

    edges = jnp.where(z < 3, 1, 0) + jnp.where(z > 0, 1, 0)
    pl.semaphore_wait(barrier, PEERS - 1 + 5 + edges)

    exps_right_going = pltpu.make_async_remote_copy(
        exps, exps_left, exps_send.at[0], exps_recv.at[0], device_id=after, device_id_type=MESH
    )
    exps_left_going = pltpu.make_async_remote_copy(
        exps, exps_right, exps_send.at[1], exps_recv.at[1], device_id=before, device_id_type=MESH
    )
    exps_right_going.start()
    exps_left_going.start()
    start_halo(0)
    relay_halo(0)

    def open_chunk(j, carry):
        load(j).start()
        return carry

    lax.fori_loop(0, CHUNKS, open_chunk, 0)
    exps_right_going.wait_recv()
    exps_left_going.wait_recv()

    not_first = jnp.where(f == 0, 0.0, 1.0).astype(jnp.float32)

    def compute(j):
        shift = wide
        keep_0 = jnp.where((f == 31) & (shift == 0), 0.0, 1.0).astype(jnp.float32)
        keep_1 = jnp.where((f == 31) & (shift == 1), 0.0, 1.0).astype(jnp.float32)
        keep = jnp.where(f == 31, 0.0, 1.0).astype(jnp.float32)
        here = jnp.exp2(exps[:, lanes(j)].astype(jnp.float32))
        left = jnp.exp2(exps_left[:, lanes(j)].astype(jnp.float32)) * not_first
        right = jnp.exp2(exps_right[:, lanes(j)].astype(jnp.float32))
        line = [left[2:3], left[3:4]] + [here[b : b + 1] for b in range(4)] + [right[0:1], right[1:2]]
        factor = [jnp.where(shift == 0, line[b], line[b + 1]) for b in range(7)]

        for k in range(2):
            def filter_rows(i, carry):
                rows = pl.ds(pl.multiple_of(i * 32, 32), 32)
                scaled = [window[j, b, k, rows, :].astype(jnp.float32) * factor[b] for b in range(7)]
                tap = [taps[q, rows, :] for q in range(4)]
                for t in range(BLOCKS):
                    if t < 2:
                        total = scaled[t] * tap[0] + scaled[t + 1] * tap[1] + scaled[t + 2] * tap[2]
                    elif t == 2:
                        total = scaled[t] * tap[0] + scaled[t + 1] * tap[1] + scaled[t + 2] * tap[2]
                        total = total * keep_1
                    else:
                        total = (scaled[t] * tap[0] + scaled[t + 1] * tap[1]) * keep
                        total = total + scaled[t + 2] * tap[2] * keep_0
                    total = total + scaled[t + 3] * tap[3]
                    filtered[pl.ds(pl.multiple_of(k * COUNT + i * 32, 32), 32),
                             t * LANES : (t + 1) * LANES] = total.astype(jnp.bfloat16)
                return carry

            lax.fori_loop(0, COUNT // 32, filter_rows, 0)

        def transform(m, carry):
            result = jnp.dot(
                table[pl.ds(pl.multiple_of(m * 256, 256), 256), :], filtered[...],
                preferred_element_type=jnp.float32,
            ) * (1.0 / (256.0 * math.sqrt(COUNT)))
            for t in range(BLOCKS):
                regroup[pl.ds(t, 256, stride=BLOCKS), :] = result[:, t * LANES : (t + 1) * LANES]
            spectra[j, pl.ds(m * 8, 8)] = regroup[...].astype(jnp.bfloat16).reshape(8, ROWS, LANES)
            return carry

        lax.fori_loop(0, 4, transform, 0)

    def own_copies(j):
        mine = y * 8 + x_hi * 4 + z
        rest = y * 8 + x2 * 4 + z
        return (
            pltpu.make_async_copy(spectra.at[j, mine], gathered.at[h, x_hi, j, me], own_sem.at[0, j]),
            pltpu.make_async_copy(spectra.at[j, rest], other.at[j, me], own_sem.at[1, j]),
        )

    def send_peers(j):
        for copy in own_copies(j):
            copy.start()

        def one(p, carry):
            py, pz, device = peer(p)
            pltpu.make_async_remote_copy(
                spectra.at[j, py * 8 + x_hi * 4 + pz], gathered.at[h, x_hi, j, me],
                peer_send.at[0, j], peer_recv.at[0, j], device_id=device, device_id_type=MESH,
            ).start()
            pltpu.make_async_remote_copy(
                spectra.at[j, py * 8 + x2 * 4 + pz], other.at[j, me],
                peer_send.at[1, j], peer_recv.at[1, j], device_id=device, device_id_type=MESH,
            ).start()
            return carry

        lax.fori_loop(1, PEERS, one, 0)

    def take(ref, sem):
        pltpu.make_async_copy(ref, ref, sem).wait()

    def wait_peers(j):
        for copy in own_copies(j):
            copy.wait()
        take(gathered.at[h, x_hi, j, pl.ds(0, PEERS - 1)], peer_recv.at[0, j])
        take(other.at[j, pl.ds(0, PEERS - 1)], peer_recv.at[1, j])

    def step(j, carry):
        @pl.when(j < CHUNKS)
        def _():
            load(j).wait()
            wait_halo(j)


            @pl.when(j + 1 < CHUNKS)
            def _():
                start_halo(j + 1)

            compute(j)
            send_peers(j)

        @pl.when((j >= 1) & (j < CHUNKS + 1))
        def _():
            i = j - 1
            wait_peers(i)
            passes[2](i).start()
            passes[0](i).start()
            passes[1](i).start()

        @pl.when(j + 1 < CHUNKS)
        def _():
            relay_halo(j + 1)

        @pl.when((j >= 2) & (j < CHUNKS + 2))
        def _():
            i = j - 2
            passes[2](i).wait_recv()
            passes[3](i).start()
            passes[4](i).start()
            passes[0](i).wait_recv()
            passes[5](i).start()

        @pl.when(j >= 3)
        def _():
            i = j - 3
            passes[3](i).wait_recv()
            passes[6](i).start()

        return carry

    lax.fori_loop(0, CHUNKS + 3, step, 0)

    def finish(j, carry):
        for kind in (1, 4, 5, 6):
            passes[kind](j).wait_recv()
        for kind in range(7):
            passes[kind](j).wait_send()
        finish_halo(j)
        take(spectra.at[j, pl.ds(0, PEERS - 1)], peer_send.at[0, j])
        take(spectra.at[j, pl.ds(0, PEERS - 1)], peer_send.at[1, j])
        return carry

    lax.fori_loop(0, CHUNKS, finish, 0)
    exps_right_going.wait_send()
    exps_left_going.wait_send()


def spread(volts, exps):
    table = jnp.asarray(dft_table(COUNT))
    taps = jnp.asarray(
        np.ascontiguousarray(
            np.broadcast_to(make_window(COUNT).reshape(4, COUNT, 1), (4, COUNT, LANES))
        )
    )
    in_vmem = pl.BlockSpec(memory_space=pltpu.VMEM)
    dma = pltpu.SemaphoreType.DMA
    return pl.pallas_call(
        spread_kernel,
        out_shape=jax.ShapeDtypeStruct((4, 2, CHUNKS, PEERS, ROWS, LANES), jnp.bfloat16),
        in_specs=[pl.BlockSpec(memory_space=pl.ANY), in_vmem, in_vmem, in_vmem],
        out_specs=pl.BlockSpec(memory_space=pl.ANY),
        scratch_shapes=[
            pltpu.VMEM((CHUNKS, 7, 2, COUNT, LANES), jnp.bfloat16),
            pltpu.VMEM((4, CHUNKS, 2, COUNT // 4, LANES), jnp.bfloat16),
            pltpu.VMEM((BLOCKS, INPUTS), jnp.int32),
            pltpu.VMEM((BLOCKS, INPUTS), jnp.int32),
            pltpu.VMEM((2 * COUNT, BLOCKS * LANES), jnp.bfloat16),
            pltpu.VMEM((256 * BLOCKS, LANES), jnp.float32),
            pltpu.VMEM((CHUNKS, 32, ROWS, LANES), jnp.bfloat16),
            pltpu.VMEM((CHUNKS, PEERS, ROWS, LANES), jnp.bfloat16),
            dma((CHUNKS,)),
            dma((4, CHUNKS)),
            dma((4, CHUNKS)),
            dma((4, CHUNKS)),
            dma((4, CHUNKS)),
            dma((2,)),
            dma((2,)),
            dma((2, CHUNKS)),
            dma((2, CHUNKS)),
            dma((2, CHUNKS)),
            dma((7, CHUNKS)),
            dma((7, CHUNKS)),
        ],
        compiler_params=pltpu.CompilerParams(
            collective_id=0, has_side_effects=True, vmem_limit_bytes=56 * 2**20
        ),
        cost_estimate=pl.CostEstimate(
            flops=8 * 2**30, bytes_accessed=50 * 2**20, transcendentals=0
        ),
    )(volts, exps, table, taps)


def correlate_kernel(spectra, out, values, left):
    half = lax.axis_index("half")
    sources = 8 * PEERS
    for u in range(CHUNKS):
        wide = spectra[:, u].astype(jnp.float32).reshape(sources, 2, 8, LANES)
        for c in range(2):
            values[c, :, u * LANES : (u + 1) * LANES] = (
                wide[:, c].reshape(sources * 8, LANES).astype(jnp.bfloat16)
            )
    sign = jnp.where(lax.broadcasted_iota(jnp.int32, (1, 8, LANES), 1) < 4, 1.0, -1.0)
    for u in range(2):
        wide = spectra[:, 2 * half + u].astype(jnp.float32).reshape(sources, 2, 8, LANES)
        for c in range(2):
            plain = wide[:, c]
            swapped = pltpu.roll(plain, 4, 1) * sign
            at = u * LANES
            left[c, :, at : at + LANES] = plain.reshape(sources * 8, LANES).astype(jnp.bfloat16)
            at = 256 + u * LANES
            left[c, :, at : at + LANES] = swapped.reshape(sources * 8, LANES).astype(jnp.bfloat16)
    for c in range(2):
        result = lax.dot_general(
            left[c], values[c], (((0,), (0,)), ((), ())), preferred_element_type=jnp.float32
        ) * (1.0 / 512.0)
        out[:, c, 0, :] = result[:256].astype(jnp.bfloat16)
        out[:, c, 1, :] = result[256:].astype(jnp.bfloat16)


def correlate(spectra):
    return pl.pallas_call(
        correlate_kernel,
        grid=(8,),
        out_shape=jax.ShapeDtypeStruct((256, 16, 2, INPUTS), jnp.bfloat16),
        in_specs=[pl.BlockSpec((8, CHUNKS, PEERS, 16, LANES), lambda i: (0, 0, 0, i, 0))],
        out_specs=pl.BlockSpec((256, 2, 2, INPUTS), lambda i: (0, i, 0, 0)),
        scratch_shapes=[
            pltpu.VMEM((2, 1024, INPUTS), jnp.bfloat16),
            pltpu.VMEM((2, 1024, 512), jnp.bfloat16),
        ],
        compiler_params=pltpu.CompilerParams(vmem_limit_bytes=56 * 2**20),
        cost_estimate=pl.CostEstimate(
            flops=16 * 2**30, bytes_accessed=48 * 2**20, transcendentals=0
        ),
    )(spectra)


def per_device(voltages, scale_exps):
    gathered = spread(voltages[0], scale_exps[0])
    return correlate(gathered.reshape(8, CHUNKS, PEERS, ROWS, LANES))


def solution(mesh):
    return jax.shard_map(
        per_device,
        mesh=mesh,
        in_specs=(P("half", "freq", None, None, None), P("half", "freq", None)),
        out_specs=P("half", "freq", None, None),
        check_vma=False,
    )
```

```python
import functools
import math

import jax
import jax.numpy as jnp
import ml_dtypes
import numpy as np
from jax import lax
from jax.experimental import pallas as pl
from jax.experimental.pallas import tpu as pltpu
from jax.sharding import PartitionSpec as P

MESH = pl.DeviceIdType.MESH
LANES = 128
COUNT = 512
INPUTS = 1024
CHUNKS = INPUTS // LANES
BLOCKS = 4
PEERS = 16
ROWS = 128


def make_window(count):
    steps = np.arange(4 * count, dtype=np.float64) + 0.5
    window = np.sinc(steps / count - 2.0) * (
        0.5 - 0.5 * np.cos(2.0 * math.pi * steps / (4 * count))
    )
    return window.astype(np.float32)


def dft_table(count):
    index = np.arange(count)
    angle = 2.0 * math.pi / count * (index[:, None] * index[None, :] % count)
    cosine, sine = np.cos(angle), np.sin(angle)
    upper = np.concatenate([cosine, sine], axis=1)
    lower = np.concatenate([-sine, cosine], axis=1)
    table = np.stack([upper, lower], axis=1).reshape(2 * count, 2 * count)
    return table.astype(np.float32).astype(ml_dtypes.bfloat16)


def spread_kernel(
    volts, exps, table, taps, gathered,
    window, relay, exps_left, exps_right, filtered, regroup, spectra, other,
    in_sem, halo_send, halo_recv, relay_send, relay_recv, exps_send, exps_recv, own_sem,
    peer_send, peer_recv, pass_send, pass_recv,
):
    f = lax.axis_index("freq")
    h = lax.axis_index("half")
    y, x_hi, z = f // 8, f // 4 % 2, f % 4
    x_lo = h // 2
    me = y * 4 + z
    after = {"freq": (f + 1) % 32, "half": h}
    before = {"freq": (f + 31) % 32, "half": h}
    partner = {"freq": f, "half": (h + 2) % 4}
    sibling = {"freq": f, "half": x_lo * 2 + (h + 1) % 2}
    across = {"freq": y * 8 + (1 - x_hi) * 4 + z, "half": (h + 2) % 4}

    def peer(p):
        py, pz = (y + p // 4) % 4, (z + p % 4) % 4
        return py, pz, {"freq": py * 8 + x_hi * 4 + pz, "half": h}

    def lanes(j):
        return pl.ds(pl.multiple_of(j * LANES, LANES), LANES)

    wide = h % 2

    def load(j):
        return pltpu.make_async_copy(
            volts.at[:, :, :, lanes(j)], window.at[j, pl.ds(2 - wide, BLOCKS)], in_sem.at[j]
        )

    halo_block = (3, 2, 0, 1)

    def place(kind, j):
        return (1 - wide, 0, 6 - wide, 6)[kind]

    edge = (3, 3, 0, 0)
    part = COUNT // 4

    def halo(kind, j):
        return pltpu.make_async_remote_copy(
            volts.at[halo_block[kind], :, :, lanes(j)], window.at[j, place(kind, j)],
            halo_send.at[kind, j], halo_recv.at[kind, j],
            device_id=after if kind < 2 else before, device_id_type=MESH,
        )

    def halo_part(kind, j, q):
        rows = pl.ds(q * part, part)
        source = volts.at[halo_block[kind], :, rows, lanes(j)]
        if q == edge[kind]:
            return pltpu.make_async_remote_copy(
                source, window.at[j, place(kind, j), :, rows],
                halo_send.at[kind, j], halo_recv.at[kind, j],
                device_id=after if kind < 2 else before, device_id_type=MESH,
            )
        return pltpu.make_async_remote_copy(
            source, relay.at[kind, j], halo_send.at[kind, j], relay_recv.at[kind, j],
            device_id={"freq": f - z + q, "half": h}, device_id_type=MESH,
        )

    def halo_from_relay(kind, j):
        beyond = (f - z + 4) % 32 if kind < 2 else (f - z + 31) % 32
        rows = pl.ds(pl.multiple_of(z * part, part), part)
        return pltpu.make_async_remote_copy(
            relay.at[kind, j], window.at[j, place(kind, j), :, rows],
            relay_send.at[kind, j], halo_recv.at[kind, j],
            device_id={"freq": beyond, "half": h}, device_id_type=MESH,
        )

    def each_kind(act):
        for kind in range(4):
            if kind % 2 == 0:
                act(kind)
            else:
                pl.when(wide == kind // 2)(functools.partial(act, kind))

    def start_halo(j):
        def act(kind):
            pl.when(z != edge[kind])(lambda: halo(kind, j).start())

            @pl.when(z == edge[kind])
            def _():
                for q in range(4):
                    halo_part(kind, j, q).start()

        each_kind(act)

    def relay_halo(j):
        def act(kind):
            @pl.when(z != edge[kind])
            def _():
                pltpu.make_async_copy(
                    relay.at[kind, j], relay.at[kind, j], relay_recv.at[kind, j]
                ).wait()
                halo_from_relay(kind, j).start()

        each_kind(act)

    def wait_halo(j):
        each_kind(lambda kind: halo(kind, j).wait_recv())

    def finish_halo(j):
        def act(kind):
            halo(kind, j).wait_send()
            pl.when(z != edge[kind])(lambda: halo_from_relay(kind, j).wait_send())

        each_kind(act)

    def passing(kind, j, source, slot_h, slot_x, target):
        return pltpu.make_async_remote_copy(
            source, gathered.at[slot_h, slot_x, j],
            pass_send.at[kind, j], pass_recv.at[kind, j], device_id=target, device_id_type=MESH,
        )

    h2, x2 = (h + 2) % 4, 1 - x_hi
    passes = (
        lambda j: passing(0, j, gathered.at[h, x_hi, j], h, x_hi, partner),
        lambda j: passing(1, j, gathered.at[h, x_hi, j], h, x_hi, sibling),
        lambda j: passing(2, j, other.at[j], h, x_hi, across),
        lambda j: passing(3, j, gathered.at[h2, x2, j], h2, x2, partner),
        lambda j: passing(4, j, gathered.at[h2, x2, j], h2, x2, sibling),
        lambda j: passing(5, j, gathered.at[h2, x_hi, j], h2, x_hi, sibling),
        lambda j: passing(6, j, gathered.at[h, x2, j], h, x2, sibling),
    )

    barrier = pltpu.get_barrier_semaphore()

    def greet(p, carry):
        pl.semaphore_signal(barrier, inc=1, device_id=peer(p)[2], device_id_type=MESH)
        return carry

    lax.fori_loop(1, PEERS, greet, 0)
    for device in (after, before, partner, sibling, across):
        pl.semaphore_signal(barrier, inc=1, device_id=device, device_id_type=MESH)
    for step_back in (2, 3, 4):
        @pl.when(z == 0)
        def _():
            device = {"freq": (f + 32 - step_back) % 32, "half": h}
            pl.semaphore_signal(barrier, inc=1, device_id=device, device_id_type=MESH)

        @pl.when(z == 3)
        def _():
            device = {"freq": (f + step_back) % 32, "half": h}
            pl.semaphore_signal(barrier, inc=1, device_id=device, device_id_type=MESH)

    edges = jnp.where(z < 3, 1, 0) + jnp.where(z > 0, 1, 0)
    pl.semaphore_wait(barrier, PEERS - 1 + 5 + edges)

    exps_right_going = pltpu.make_async_remote_copy(
        exps, exps_left, exps_send.at[0], exps_recv.at[0], device_id=after, device_id_type=MESH
    )
    exps_left_going = pltpu.make_async_remote_copy(
        exps, exps_right, exps_send.at[1], exps_recv.at[1], device_id=before, device_id_type=MESH
    )
    exps_right_going.start()
    exps_left_going.start()
    start_halo(0)
    relay_halo(0)

    def open_chunk(j, carry):
        load(j).start()
        return carry

    lax.fori_loop(0, CHUNKS, open_chunk, 0)
    exps_right_going.wait_recv()
    exps_left_going.wait_recv()

    not_first = jnp.where(f == 0, 0.0, 1.0).astype(jnp.float32)

    def compute(j):
        shift = wide
        keep_0 = jnp.where((f == 31) & (shift == 0), 0.0, 1.0).astype(jnp.float32)
        keep_1 = jnp.where((f == 31) & (shift == 1), 0.0, 1.0).astype(jnp.float32)
        keep = jnp.where(f == 31, 0.0, 1.0).astype(jnp.float32)
        here = jnp.exp2(exps[:, lanes(j)].astype(jnp.float32))
        left = jnp.exp2(exps_left[:, lanes(j)].astype(jnp.float32)) * not_first
        right = jnp.exp2(exps_right[:, lanes(j)].astype(jnp.float32))
        line = [left[2:3], left[3:4]] + [here[b : b + 1] for b in range(4)] + [right[0:1], right[1:2]]
        factor = [jnp.where(shift == 0, line[b], line[b + 1]) for b in range(7)]

        for k in range(2):
            def filter_rows(i, carry):
                rows = pl.ds(pl.multiple_of(i * 32, 32), 32)
                scaled = [window[j, b, k, rows, :].astype(jnp.float32) * factor[b] for b in range(7)]
                tap = [taps[q, rows, :] for q in range(4)]
                for t in range(BLOCKS):
                    if t < 2:
                        total = scaled[t] * tap[0] + scaled[t + 1] * tap[1] + scaled[t + 2] * tap[2]
                    elif t == 2:
                        total = scaled[t] * tap[0] + scaled[t + 1] * tap[1] + scaled[t + 2] * tap[2]
                        total = total * keep_1
                    else:
                        total = (scaled[t] * tap[0] + scaled[t + 1] * tap[1]) * keep
                        total = total + scaled[t + 2] * tap[2] * keep_0
                    total = total + scaled[t + 3] * tap[3]
                    filtered[pl.ds(pl.multiple_of(k * COUNT + i * 32, 32), 32),
                             t * LANES : (t + 1) * LANES] = total.astype(jnp.bfloat16)
                return carry

            lax.fori_loop(0, COUNT // 32, filter_rows, 0)

        def transform(m, carry):
            result = jnp.dot(
                table[pl.ds(pl.multiple_of(m * 256, 256), 256), :], filtered[...],
                preferred_element_type=jnp.float32,
            ) * (1.0 / (256.0 * math.sqrt(COUNT)))
            for t in range(BLOCKS):
                regroup[pl.ds(t, 256, stride=BLOCKS), :] = result[:, t * LANES : (t + 1) * LANES]
            spectra[j, pl.ds(m * 8, 8)] = regroup[...].astype(jnp.bfloat16).reshape(8, ROWS, LANES)
            return carry

        lax.fori_loop(0, 4, transform, 0)

    def own_copies(j):
        mine = y * 8 + x_hi * 4 + z
        rest = y * 8 + x2 * 4 + z
        return (
            pltpu.make_async_copy(spectra.at[j, mine], gathered.at[h, x_hi, j, me], own_sem.at[0, j]),
            pltpu.make_async_copy(spectra.at[j, rest], other.at[j, me], own_sem.at[1, j]),
        )

    def send_peers(j):
        for copy in own_copies(j):
            copy.start()

        def one(p, carry):
            py, pz, device = peer(p)
            pltpu.make_async_remote_copy(
                spectra.at[j, py * 8 + x2 * 4 + pz], other.at[j, me],
                peer_send.at[1, j], peer_recv.at[1, j], device_id=device, device_id_type=MESH,
            ).start()
            return carry

        lax.fori_loop(1, PEERS, one, 0)

        def two(p, carry):
            py, pz, device = peer(p)
            pltpu.make_async_remote_copy(
                spectra.at[j, py * 8 + x_hi * 4 + pz], gathered.at[h, x_hi, j, me],
                peer_send.at[0, j], peer_recv.at[0, j], device_id=device, device_id_type=MESH,
            ).start()
            return carry

        lax.fori_loop(1, PEERS, two, 0)

    def take(ref, sem):
        pltpu.make_async_copy(ref, ref, sem).wait()

    def wait_peers(j):
        for copy in own_copies(j):
            copy.wait()
        take(gathered.at[h, x_hi, j, pl.ds(0, PEERS - 1)], peer_recv.at[0, j])
        take(other.at[j, pl.ds(0, PEERS - 1)], peer_recv.at[1, j])

    def step(j, carry):
        @pl.when(j < CHUNKS)
        def _():
            load(j).wait()
            wait_halo(j)


            @pl.when(j + 1 < CHUNKS)
            def _():
                start_halo(j + 1)

        @pl.when((j >= 1) & (j < CHUNKS + 1))
        def _():
            i = j - 1
            wait_peers(i)
            passes[2](i).start()
            passes[0](i).start()
            passes[1](i).start()

        @pl.when(j < CHUNKS)
        def _():
            compute(j)
            send_peers(j)

        @pl.when(j + 1 < CHUNKS)
        def _():
            relay_halo(j + 1)

        @pl.when((j >= 2) & (j < CHUNKS + 2))
        def _():
            i = j - 2
            passes[2](i).wait_recv()
            passes[3](i).start()
            passes[4](i).start()
            passes[0](i).wait_recv()
            passes[5](i).start()

        @pl.when(j >= 3)
        def _():
            i = j - 3
            passes[3](i).wait_recv()
            passes[6](i).start()

        return carry

    lax.fori_loop(0, CHUNKS + 3, step, 0)

    def finish(j, carry):
        for kind in (1, 4, 5, 6):
            passes[kind](j).wait_recv()
        for kind in range(7):
            passes[kind](j).wait_send()
        finish_halo(j)
        take(spectra.at[j, pl.ds(0, PEERS - 1)], peer_send.at[0, j])
        take(spectra.at[j, pl.ds(0, PEERS - 1)], peer_send.at[1, j])
        return carry

    lax.fori_loop(0, CHUNKS, finish, 0)
    exps_right_going.wait_send()
    exps_left_going.wait_send()


def spread(volts, exps):
    table = jnp.asarray(dft_table(COUNT))
    taps = jnp.asarray(
        np.ascontiguousarray(
            np.broadcast_to(make_window(COUNT).reshape(4, COUNT, 1), (4, COUNT, LANES))
        )
    )
    in_vmem = pl.BlockSpec(memory_space=pltpu.VMEM)
    dma = pltpu.SemaphoreType.DMA
    return pl.pallas_call(
        spread_kernel,
        out_shape=jax.ShapeDtypeStruct((4, 2, CHUNKS, PEERS, ROWS, LANES), jnp.bfloat16),
        in_specs=[pl.BlockSpec(memory_space=pl.ANY), in_vmem, in_vmem, in_vmem],
        out_specs=pl.BlockSpec(memory_space=pl.ANY),
        scratch_shapes=[
            pltpu.VMEM((CHUNKS, 7, 2, COUNT, LANES), jnp.bfloat16),
            pltpu.VMEM((4, CHUNKS, 2, COUNT // 4, LANES), jnp.bfloat16),
            pltpu.VMEM((BLOCKS, INPUTS), jnp.int32),
            pltpu.VMEM((BLOCKS, INPUTS), jnp.int32),
            pltpu.VMEM((2 * COUNT, BLOCKS * LANES), jnp.bfloat16),
            pltpu.VMEM((256 * BLOCKS, LANES), jnp.float32),
            pltpu.VMEM((CHUNKS, 32, ROWS, LANES), jnp.bfloat16),
            pltpu.VMEM((CHUNKS, PEERS, ROWS, LANES), jnp.bfloat16),
            dma((CHUNKS,)),
            dma((4, CHUNKS)),
            dma((4, CHUNKS)),
            dma((4, CHUNKS)),
            dma((4, CHUNKS)),
            dma((2,)),
            dma((2,)),
            dma((2, CHUNKS)),
            dma((2, CHUNKS)),
            dma((2, CHUNKS)),
            dma((7, CHUNKS)),
            dma((7, CHUNKS)),
        ],
        compiler_params=pltpu.CompilerParams(
            collective_id=0, has_side_effects=True, vmem_limit_bytes=56 * 2**20
        ),
        cost_estimate=pl.CostEstimate(
            flops=8 * 2**30, bytes_accessed=50 * 2**20, transcendentals=0
        ),
    )(volts, exps, table, taps)


def correlate_kernel(spectra, out, values, left):
    half = lax.axis_index("half")
    sources = 8 * PEERS
    for u in range(CHUNKS):
        wide = spectra[:, u].astype(jnp.float32).reshape(sources, 2, 8, LANES)
        for c in range(2):
            values[c, :, u * LANES : (u + 1) * LANES] = (
                wide[:, c].reshape(sources * 8, LANES).astype(jnp.bfloat16)
            )
    sign = jnp.where(lax.broadcasted_iota(jnp.int32, (1, 8, LANES), 1) < 4, 1.0, -1.0)
    for u in range(2):
        wide = spectra[:, 2 * half + u].astype(jnp.float32).reshape(sources, 2, 8, LANES)
        for c in range(2):
            plain = wide[:, c]
            swapped = pltpu.roll(plain, 4, 1) * sign
            at = u * LANES
            left[c, :, at : at + LANES] = plain.reshape(sources * 8, LANES).astype(jnp.bfloat16)
            at = 256 + u * LANES
            left[c, :, at : at + LANES] = swapped.reshape(sources * 8, LANES).astype(jnp.bfloat16)
    for c in range(2):
        result = lax.dot_general(
            left[c], values[c], (((0,), (0,)), ((), ())), preferred_element_type=jnp.float32
        ) * (1.0 / 512.0)
        out[:, c, 0, :] = result[:256].astype(jnp.bfloat16)
        out[:, c, 1, :] = result[256:].astype(jnp.bfloat16)


def correlate(spectra):
    return pl.pallas_call(
        correlate_kernel,
        grid=(8,),
        out_shape=jax.ShapeDtypeStruct((256, 16, 2, INPUTS), jnp.bfloat16),
        in_specs=[pl.BlockSpec((8, CHUNKS, PEERS, 16, LANES), lambda i: (0, 0, 0, i, 0))],
        out_specs=pl.BlockSpec((256, 2, 2, INPUTS), lambda i: (0, i, 0, 0)),
        scratch_shapes=[
            pltpu.VMEM((2, 1024, INPUTS), jnp.bfloat16),
            pltpu.VMEM((2, 1024, 512), jnp.bfloat16),
        ],
        compiler_params=pltpu.CompilerParams(vmem_limit_bytes=56 * 2**20),
        cost_estimate=pl.CostEstimate(
            flops=16 * 2**30, bytes_accessed=48 * 2**20, transcendentals=0
        ),
    )(spectra)


def per_device(voltages, scale_exps):
    gathered = spread(voltages[0], scale_exps[0])
    return correlate(gathered.reshape(8, CHUNKS, PEERS, ROWS, LANES))


def solution(mesh):
    return jax.shard_map(
        per_device,
        mesh=mesh,
        in_specs=(P("half", "freq", None, None, None), P("half", "freq", None)),
        out_specs=P("half", "freq", None, None),
        check_vma=False,
    )
```
